32 devices in a mesh: section: 2 (over core), dp: 16 (over z, y, x).
Axes of the slice: x: 2, y: 2, z: 4, core: 2. Of those that a mesh axis runs over, the one named last changes fastest.
Arguments:
- inputs: bfloat16 [4, 512, 4096], P(None, 'dp'), may hold values from -8 to 8
- cotangent: bfloat16 [4, 512, 4096], P(None, 'dp'), may hold values from -0.125 to 0.125
- weight: bfloat16 [2, 4096, 512], P('section'), may hold values from -0.09375 to 0.09375
- gain: bfloat16 [2, 4096], P('section'), may hold values from 0.099609375 to 1.8984375
Outputs:
- weight_grad: float32 [2, 4096, 512], P('section', 'dp')
- gain_grad: float32 [2, 4096], P('section', 'dp')
The draws below stay inside these ranges and needn't reach their ends.
All inputs are finite; a program needn't handle non-finite values.
Results may differ from the reference program's by a relative error of at most 0.017.
Values may be sent and summed in bfloat16 or wider, within the bound.
A program may use at most 128 MiB of HBM per device.

```python
import jax
import jax.numpy as jnp
from jax import lax

D = 4096
KV_WIDTH = 512
MB = 4
MB_ROWS = 32
TOKENS = 512
SECTIONS = 2
N_DP = 16


def raised(drawn, own_key, source, target, blocks, factor):
    def block_of(dim):
        return (jnp.arange(drawn.shape[dim]) // (drawn.shape[dim] // blocks)).reshape((-1,) + (1,) * (drawn.ndim - 1 - dim))

    first = jax.random.permutation(own_key, blocks)[block_of(target)]
    second = (block_of(target) + blocks // 2) % blocks
    return jnp.where((block_of(source) == first) | (block_of(source) == second), factor * drawn, drawn)


def block_scale(stream_key, dims, pieces, smallest, high):
    level = 1.0
    for dim, blocks in pieces:
        steps = jax.random.uniform(jax.random.fold_in(jax.random.fold_in(stream_key, 6), dim), (blocks,), jnp.float32, smallest / len(pieces), high / len(pieces))
        level = level * jnp.repeat(jnp.exp(steps), dims[dim] // blocks).reshape((-1,) + (1,) * (len(dims) - 1 - dim))
    return level


def normal_values(rng, shape, width, limit, shards=(), kind=jnp.bfloat16):
    level = block_scale(rng, shape, shards, -0.22, 0.18) if shards else 1.0
    entries = jax.random.normal(rng, shape, jnp.float32) * width * level
    return jnp.minimum(jnp.maximum(entries, -limit), limit).astype(kind)


def bell_draw_with(rng, extent, width, bound, shards, heavy, kind=jnp.bfloat16):
    result = width * jax.random.normal(rng, extent, jnp.float32)
    if shards:
        result = result * block_scale(rng, extent, shards, -0.22, 0.18)
    return jnp.clip(raised(result, jax.random.fold_in(rng, 3), *heavy), -bound, bound).astype(kind)


def setup_inputs(seed: int = 0) -> dict:
    key_list = jax.random.split(jax.random.key(seed), 5)
    inputs = bell_draw_with(key_list[0], (MB, TOKENS, D), 1.0, 8.0, ((1, 16),), (1, 2, 16, 2.0))
    cotangent = normal_values(key_list[1], (MB, TOKENS, D), ((MB * TOKENS) ** -0.5), 0.125, ((1, 16),))
    weight = normal_values(key_list[2], (SECTIONS, D, KV_WIDTH), D ** -0.5, 0.09375, ((0, 2),))
    gain = jnp.clip(1.0 + 0.18 * jax.random.normal(key_list[3], (SECTIONS, D), jnp.float32), 0.099609375, 1.8984375).astype(jnp.bfloat16)
    return {"inputs": inputs, "cotangent": cotangent, "weight": weight, "gain": gain}


EPSILON = 1e-05

def layer_forward(values, gain_row, weights):
    wide = values.astype(jnp.float32)
    inv_rms = lax.rsqrt(lax.optimization_barrier(jnp.mean(wide * wide, axis=-1, keepdims=True)) + EPSILON)
    normed = (wide * inv_rms * gain_row.astype(jnp.float32)).astype(jnp.bfloat16)
    hidden = jnp.dot(normed, weights, preferred_element_type=jnp.float32)
    active = jax.nn.silu(hidden).astype(jnp.bfloat16)
    back_proj = lax.dot_general(active, weights, (((1,), (1,)), ((), ())), preferred_element_type=jnp.float32)
    return ((wide + back_proj).astype(jnp.bfloat16), hidden)

def layer_backward(values, hidden, upstream, gain_row, weights):
    wide = values.astype(jnp.float32)
    gain_wide = gain_row.astype(jnp.float32)
    inv_rms = lax.rsqrt(lax.optimization_barrier(jnp.mean(wide * wide, axis=-1, keepdims=True)) + EPSILON)
    unit_rows = wide * inv_rms
    normed = (unit_rows * gain_wide).astype(jnp.bfloat16)
    logistic = jax.nn.sigmoid(hidden)
    active = jax.nn.silu(hidden).astype(jnp.bfloat16)
    grad_w = lax.dot_general(upstream, active, (((0,), (0,)), ((), ())), preferred_element_type=jnp.float32)
    d_active = jnp.dot(upstream, weights, preferred_element_type=jnp.float32)
    d_hidden = (d_active * logistic * (1.0 + hidden * (1.0 - logistic))).astype(jnp.bfloat16)
    grad_w = grad_w + lax.dot_general(normed, d_hidden, (((0,), (0,)), ((), ())), preferred_element_type=jnp.float32)
    d_normed = lax.dot_general(d_hidden, weights, (((1,), (1,)), ((), ())), preferred_element_type=jnp.float32)
    grad_g = lax.optimization_barrier(jnp.sum(d_normed * unit_rows, axis=0))
    d_unit = d_normed * gain_wide
    d_values = inv_rms * (d_unit - unit_rows * lax.optimization_barrier(jnp.mean(d_unit * unit_rows, axis=-1, keepdims=True)))
    return ((upstream.astype(jnp.float32) + d_values).astype(jnp.bfloat16), grad_w, grad_g)

def pipe_grads(block_in, block_ct, weight, gain):
    count = block_in.shape[0] * block_in.shape[1]
    values = block_in.reshape(count, block_in.shape[2])
    saved = []
    for layer in range(SECTIONS):
        output, hidden = layer_forward(values, gain[layer], weight[layer])
        saved.append((values, hidden))
        values = output
    upstream = block_ct.reshape(count, block_ct.shape[2])
    grads_w = []
    grads_g = []
    for layer in range(SECTIONS - 1, -1, -1):
        upstream, grad_w, grad_g = layer_backward(saved[layer][0], saved[layer][1], upstream, gain[layer], weight[layer])
        grads_w.append(grad_w)
        grads_g.append(grad_g)
    return (jnp.stack(grads_w[::-1]), jnp.stack(grads_g[::-1]))

def rounded(value):
    return lax.optimization_barrier(value.astype(jnp.bfloat16)).astype(jnp.float32)

def reference(inputs, cotangent, weight, gain):
    per_pipe = MB // 2
    grouped_in = inputs.reshape(MB, N_DP, MB_ROWS, D)
    grouped_ct = cotangent.reshape(MB, N_DP, MB_ROWS, D)

    def replica_step(carry, index):
        total_w, total_g = carry
        block_in = lax.dynamic_index_in_dim(grouped_in, index, 1, keepdims=False)
        block_ct = lax.dynamic_index_in_dim(grouped_ct, index, 1, keepdims=False)
        first_w, first_g = pipe_grads(block_in[:per_pipe], block_ct[:per_pipe], weight, gain)
        second_w, second_g = pipe_grads(block_in[per_pipe:], block_ct[per_pipe:], weight, gain)
        total_w = total_w + rounded(first_w) + rounded(second_w)
        total_g = total_g + rounded(first_g) + rounded(second_g)
        return ((total_w, total_g), None)
    start_w = jnp.zeros((SECTIONS, D, KV_WIDTH), jnp.float32)
    start_g = jnp.zeros((SECTIONS, D), jnp.float32)
    (total_w, total_g), leftover = lax.scan(replica_step, (start_w, start_g), jnp.arange(N_DP, dtype=jnp.int32))
    return (total_w, total_g)
```

```python
import functools

import jax
import jax.numpy as jnp
from jax import lax
from jax.experimental import pallas as pl
from jax.experimental.pallas import tpu as pltpu
from jax.sharding import PartitionSpec as P

EPSILON = 1e-05
MESH = pl.DeviceIdType.MESH
LANES = 128


def part_plan(shard, bits):
    unit = shard // 8
    near, far = [0, 1], list(range(2, bits))
    return [
        (0, 3 * unit, near + far),
        (3 * unit, 3 * unit, near[::-1] + far),
        (6 * unit, unit, far + near),
        (7 * unit, unit, far + near[::-1]),
    ]


def chunk_of(depth):
    return min(512, depth)


def relay_kernel(
    sections,
    replicas,
    x_hbm,
    ct_hbm,
    w_hbm,
    gain_ref,
    out_w,
    out_g,
    w_buf,
    v_buf,
    cn_buf,
    ad_buf,
    hid_buf,
    dact_buf,
    y_buf,
    up_buf,
    dn_buf,
    r_buf,
    part_w,
    land_w,
    part_g,
    land_g,
    x_sem,
    ct_sem,
    w_sem,
    y_send,
    y_recv,
    up_send,
    up_recv,
    rs_send,
    rs_recv,
):
    section = lax.axis_index("section")
    me = lax.axis_index("dp")
    chunks, rows, width = v_buf.shape
    depth = chunks * width
    bits = replicas.bit_length() - 1
    shard = depth // replicas
    is_first = section == 0
    is_last = section == sections - 1
    my_bit = [(me // (1 << b)) % 2 for b in range(bits)]
    partner = [me + (1 - 2 * my_bit[b]) * (1 << b) for b in range(bits)]

    def x_copy(c):
        return pltpu.make_async_copy(
            x_hbm.at[:, pl.ds(pl.multiple_of(c * width, width), width)], v_buf.at[c], x_sem.at[c]
        )

    def ct_copy(c):
        return pltpu.make_async_copy(
            ct_hbm.at[:, pl.ds(pl.multiple_of(c * width, width), width)],
            cn_buf.at[c, pl.ds(0, rows)],
            ct_sem.at[c],
        )

    def w_copy(c):
        return pltpu.make_async_copy(w_hbm.at[c], w_buf.at[c], w_sem.at[c])

    @pl.when(is_first)
    def _():
        for c in range(chunks):
            x_copy(c).start()

    @pl.when(is_last)
    def _():
        for c in range(chunks):
            ct_copy(c).start()

    for c in range(chunks):
        w_copy(c).start()

    barrier = pltpu.get_barrier_semaphore()
    for b in range(bits):
        pl.semaphore_signal(barrier, inc=1, device_id=(section, partner[b]), device_id_type=MESH)

    @pl.when(jnp.logical_not(is_first))
    def _():
        pl.semaphore_signal(barrier, inc=1, device_id=(section - 1, me), device_id_type=MESH)

    @pl.when(jnp.logical_not(is_last))
    def _():
        pl.semaphore_signal(barrier, inc=1, device_id=(section + 1, me), device_id_type=MESH)

    peers = bits + jnp.where(is_first, 0, 1) + jnp.where(is_last, 0, 1)
    pl.semaphore_wait(barrier, peers)

    def y_copy(c, to):
        return pltpu.make_async_remote_copy(
            src_ref=y_buf.at[c],
            dst_ref=v_buf.at[c],
            send_sem=y_send.at[c],
            recv_sem=y_recv.at[c],
            device_id=(to, me),
            device_id_type=MESH,
        )

    def up_copy(c, to):
        return pltpu.make_async_remote_copy(
            src_ref=up_buf.at[c],
            dst_ref=cn_buf.at[c, pl.ds(0, rows)],
            send_sem=up_send.at[c],
            recv_sem=up_recv.at[c],
            device_id=(to, me),
            device_id_type=MESH,
        )

    def each_chunk(body):
        def step(c, carry):
            body(c)
            return carry

        lax.fori_loop(0, chunks, step, 0)

    def gain_of(c):
        return gain_ref[c].astype(jnp.float32)

    def add_d_active(c):
        up = cn_buf[c, pl.ds(0, rows), :]
        dact_buf[...] += jnp.dot(up, w_buf[c], preferred_element_type=jnp.float32)

    for c in range(chunks):
        w_copy(c).wait()

    dact_buf[...] = jnp.zeros_like(dact_buf)

    @pl.when(is_last)
    def _():
        def body(c):
            ct_copy(c).wait()
            add_d_active(c)

        each_chunk(body)

    def squares(c, total):
        @pl.when(is_first)
        def _():
            x_copy(c).wait()

        @pl.when(jnp.logical_not(is_first))
        def _():
            y_copy(c, section - 1).wait_recv()

        wide = v_buf[c].astype(jnp.float32)
        return total + jnp.sum(wide * wide, axis=-1, keepdims=True)

    total = lax.fori_loop(0, chunks, squares, jnp.zeros((rows, 1), jnp.float32))
    r_buf[...] = lax.rsqrt(total / depth + EPSILON)
    hid_buf[...] = jnp.zeros_like(hid_buf)

    def project(c):
        normed = (v_buf[c].astype(jnp.float32) * r_buf[...] * gain_of(c)).astype(jnp.bfloat16)
        cn_buf[c, pl.ds(rows, rows), :] = normed
        hid_buf[...] += jnp.dot(normed, w_buf[c], preferred_element_type=jnp.float32)

    each_chunk(project)
    hidden = hid_buf[...]
    ad_buf[pl.ds(0, rows), :] = (hidden * jax.nn.sigmoid(hidden)).astype(jnp.bfloat16)

    @pl.when(jnp.logical_not(is_last))
    def _():
        def body(c):
            back = lax.dot_general(
                ad_buf[pl.ds(0, rows), :],
                w_buf[c],
                (((1,), (1,)), ((), ())),
                preferred_element_type=jnp.float32,
            )
            y_buf[c] = (v_buf[c].astype(jnp.float32) + back).astype(jnp.bfloat16)
            y_copy(c, section + 1).start()

        each_chunk(body)

        def arrived(c):
            up_copy(c, section + 1).wait_recv()
            add_d_active(c)

        each_chunk(arrived)

    hidden = hid_buf[...]
    logistic = jax.nn.sigmoid(hidden)
    ad_buf[pl.ds(rows, rows), :] = (
        dact_buf[...] * logistic * (1.0 + hidden * (1.0 - logistic))
    ).astype(jnp.bfloat16)

    per_chunk = width // shard
    plan = part_plan(shard, bits)
    gain_part = len(plan)

    def block_at(order, rel):
        index = 0
        for b, r in zip(order, rel):
            index = index + (my_bit[b] + r * (1 - 2 * my_bit[b])) * (1 << b)
        return index

    def slot_of(rel, step):
        slot = sum(1 << (bits - 1 - s) for s in range(step))
        for r in rel[step + 1 :]:
            step += 1
            slot += r << (bits - 1 - step)
        return slot

    def grad_block(j):
        c, at = j // per_chunk, j % per_chunk
        left = cn_buf[c, :, pl.ds(pl.multiple_of(at * shard, shard), shard)]
        block = lax.dot_general(
            left, ad_buf[...], (((0,), (0,)), ((), ())), preferred_element_type=jnp.float32
        )
        part_w[j] = block.astype(jnp.bfloat16)

    def views(part, j, slot):
        if part == gain_part:
            return part_g.at[j], land_g.at[slot]
        at, size, _ = plan[part]
        return part_w.at[j, pl.ds(at, size)], land_w.at[slot, pl.ds(at, size)]

    def order_of(part):
        return plan[part][2] if part < gain_part else plan[0][2]

    def hop(part, rel):
        order = order_of(part)
        step = rel.index(1)
        slot = slot_of(rel, step)
        source, target = views(part, block_at(order, rel), slot)
        return pltpu.make_async_remote_copy(
            src_ref=source,
            dst_ref=target,
            send_sem=rs_send.at[part, slot],
            recv_sem=rs_recv.at[part, slot],
            device_id=(section, partner[order[step]]),
            device_id_type=MESH,
        )

    def arrivals(part, rel, steps):
        order = order_of(part)
        own = views(part, block_at(order, rel), 0)[0]
        value = own[...].astype(jnp.float32)
        for s in range(steps):
            came = rel[:s] + (1,) + rel[s + 1 :]
            hop(part, came).wait_recv()
            value = value + views(part, 0, slot_of(came, s))[1][...].astype(jnp.float32)
        return own, value

    def combos(count):
        return [tuple((n >> (count - 1 - i)) & 1 for i in range(count)) for n in range((1 << count) - 1, -1, -1)]

    far_combos = combos(bits - 2)

    def grad_group(near):
        def step(n, carry):
            rel = list(near)
            left = (1 << (bits - 2)) - 1 - n
            for i in range(bits - 2):
                rel.append((left // (1 << (bits - 3 - i))) % 2)
            grad_block(block_at(list(range(bits)), rel))
            return carry

        lax.fori_loop(0, 1 << (bits - 2), step, 0)
        for far in far_combos:
            whole = near + far
            for part in range(gain_part):
                rel = tuple(whole[b] for b in order_of(part))
                if rel[0] == 1:
                    hop(part, rel).start()

    grad_group((1, 1))

    def through(c, total):
        dn = lax.dot_general(
            ad_buf[pl.ds(rows, rows), :],
            w_buf[c],
            (((1,), (1,)), ((), ())),
            preferred_element_type=jnp.float32,
        )
        unit = v_buf[c].astype(jnp.float32) * r_buf[...]
        both = dn * unit
        gain_sum = jnp.sum(both, axis=0, keepdims=True)
        pieces = shard // LANES
        at = lax.broadcasted_iota(jnp.int32, part_g.shape[1:], 0)
        for k in range(per_chunk):
            tile = jnp.zeros(part_g.shape[1:], jnp.float32)
            for p in range(pieces):
                piece = gain_sum[:, k * shard + p * LANES : k * shard + (p + 1) * LANES]
                tile = jnp.where(at == p, jnp.broadcast_to(piece, tile.shape), tile)
            part_g[c * per_chunk + k] = tile.astype(jnp.bfloat16)
        scaled = dn * gain_of(c)
        dn_buf[c] = scaled
        return total + jnp.sum(scaled * unit, axis=-1, keepdims=True)

    total = lax.fori_loop(0, chunks, through, jnp.zeros((rows, 1), jnp.float32))

    @pl.when(jnp.logical_not(is_first))
    def _():
        mean = total / depth

        def body(c):
            unit = v_buf[c].astype(jnp.float32) * r_buf[...]
            up = cn_buf[c, pl.ds(0, rows), :].astype(jnp.float32)
            up_buf[c] = (up + r_buf[...] * (dn_buf[c] - unit * mean)).astype(jnp.bfloat16)
            up_copy(c, section - 1).start()

        each_chunk(body)

    grad_group((1, 0))
    grad_group((0, 1))
    grad_group((0, 0))
    for rest in combos(bits - 1):
        hop(gain_part, (1,) + rest).start()

    for step in range(1, bits):
        for rest in combos(bits - 1 - step):
            rel = (0,) * step + (1,) + rest
            for part in range(gain_part + 1):
                own, value = arrivals(part, rel, step)
                own[...] = value.astype(jnp.bfloat16)
                hop(part, rel).start()
    for part in range(gain_part + 1):
        _, value = arrivals(part, (0,) * bits, bits)
        if part < gain_part:
            at, size, _ = plan[part]
            out_w[pl.ds(at, size), :] = value
        else:
            for p in range(shard // LANES):
                out_g[:, p * LANES : (p + 1) * LANES] = value[p : p + 1, :]

    for part in range(gain_part + 1):
        for step in range(bits):
            for rest in combos(bits - 1 - step):
                hop(part, (0,) * step + (1,) + rest).wait_send()

    @pl.when(jnp.logical_not(is_last))
    def _():
        for c in range(chunks):
            y_copy(c, section + 1).wait_send()

    @pl.when(jnp.logical_not(is_first))
    def _():
        for c in range(chunks):
            up_copy(c, section - 1).wait_send()


def on_device(inputs, cotangent, weight, gain):
    sections, replicas = lax.axis_size("section"), lax.axis_size("dp")
    depth, kv = weight.shape[1:]
    rows = inputs.shape[0] * inputs.shape[1]
    width = chunk_of(depth)
    chunks = depth // width
    shard = depth // replicas
    bf16, f32 = jnp.bfloat16, jnp.float32
    dma = pltpu.SemaphoreType.DMA
    parts = len(part_plan(shard, replicas.bit_length() - 1)) + 1
    vmem = pl.BlockSpec(memory_space=pltpu.VMEM)
    hbm = pl.BlockSpec(memory_space=pl.ANY)
    grad_w, grad_g = pl.pallas_call(
        functools.partial(relay_kernel, sections, replicas),
        out_shape=(
            jax.ShapeDtypeStruct((shard, kv), f32),
            jax.ShapeDtypeStruct((1, shard), f32),
        ),
        in_specs=[hbm, hbm, hbm, vmem],
        out_specs=(vmem, vmem),
        scratch_shapes=[
            pltpu.VMEM((chunks, width, kv), bf16),
            pltpu.VMEM((chunks, rows, width), bf16),
            pltpu.VMEM((chunks, 2 * rows, width), bf16),
            pltpu.VMEM((2 * rows, kv), bf16),
            pltpu.VMEM((rows, kv), f32),
            pltpu.VMEM((rows, kv), f32),
            pltpu.VMEM((chunks, rows, width), bf16),
            pltpu.VMEM((chunks, rows, width), bf16),
            pltpu.VMEM((chunks, rows, width), f32),
            pltpu.VMEM((rows, 1), f32),
            pltpu.VMEM((replicas, shard, kv), bf16),
            pltpu.VMEM((replicas - 1, shard, kv), bf16),
            pltpu.VMEM((replicas, 16, LANES), bf16),
            pltpu.VMEM((replicas - 1, 16, LANES), bf16),
            dma((chunks,)),
            dma((chunks,)),
            dma((chunks,)),
            dma((chunks,)),
            dma((chunks,)),
            dma((chunks,)),
            dma((chunks,)),
            dma((parts, replicas - 1)),
            dma((parts, replicas - 1)),
        ],
        compiler_params=pltpu.CompilerParams(
            collective_id=0, has_side_effects=True, vmem_limit_bytes=50 * 1024 * 1024
        ),
        name="relay",
    )(
        inputs.reshape(rows, depth),
        cotangent.reshape(rows, depth),
        weight.reshape(chunks, width, kv),
        gain.reshape(chunks, 1, width),
    )
    return grad_w[None], grad_g


def solution(mesh):
    placed = (
        P(None, "dp", None),
        P(None, "dp", None),
        P("section", None, None),
        P("section", None),
    )
    return jax.shard_map(
        on_device,
        mesh=mesh,
        in_specs=placed,
        out_specs=(P("section", "dp", None), P("section", "dp")),
        check_vma=False,
    )
```

```python
import functools

import jax
import jax.numpy as jnp
from jax import lax
from jax.experimental import pallas as pl
from jax.experimental.pallas import tpu as pltpu
from jax.sharding import PartitionSpec as P

EPSILON = 1e-05
MESH = pl.DeviceIdType.MESH
LANES = 128


def part_plan(shard, bits):
    unit = shard // 8
    near, far = [0, 1], list(range(2, bits))
    return [
        (0, 3 * unit, near + far),
        (3 * unit, 3 * unit, near[::-1] + far),
        (6 * unit, unit, far + near),
        (7 * unit, unit, far + near[::-1]),
    ]


def chunk_of(depth):
    return min(512, depth)


def relay_kernel(
    sections,
    replicas,
    x_hbm,
    ct_hbm,
    w_hbm,
    gain_ref,
    out_w,
    out_g,
    w_buf,
    v_buf,
    cn_buf,
    ad_buf,
    hid_buf,
    dact_buf,
    y_buf,
    up_buf,
    dn_buf,
    r_buf,
    part_w,
    land_w,
    part_g,
    land_g,
    x_sem,
    ct_sem,
    w_sem,
    y_send,
    y_recv,
    up_send,
    up_recv,
    rs_send,
    rs_recv,
):
    section = lax.axis_index("section")
    me = lax.axis_index("dp")
    chunks, rows, width = v_buf.shape
    depth = chunks * width
    bits = replicas.bit_length() - 1
    shard = depth // replicas
    is_first = section == 0
    is_last = section == sections - 1
    my_bit = [(me // (1 << b)) % 2 for b in range(bits)]
    partner = [me + (1 - 2 * my_bit[b]) * (1 << b) for b in range(bits)]

    def x_copy(c):
        return pltpu.make_async_copy(
            x_hbm.at[:, pl.ds(pl.multiple_of(c * width, width), width)], v_buf.at[c], x_sem.at[c]
        )

    def ct_copy(c):
        return pltpu.make_async_copy(
            ct_hbm.at[:, pl.ds(pl.multiple_of(c * width, width), width)],
            cn_buf.at[c, pl.ds(0, rows)],
            ct_sem.at[c],
        )

    def w_copy(c):
        return pltpu.make_async_copy(w_hbm.at[c], w_buf.at[c], w_sem.at[c])

    @pl.when(is_first)
    def _():
        for c in range(chunks):
            x_copy(c).start()

    @pl.when(is_last)
    def _():
        for c in range(chunks):
            ct_copy(c).start()

    for c in range(chunks):
        w_copy(c).start()

    barrier = pltpu.get_barrier_semaphore()
    for b in range(bits):
        pl.semaphore_signal(barrier, inc=1, device_id=(section, partner[b]), device_id_type=MESH)

    @pl.when(jnp.logical_not(is_first))
    def _():
        pl.semaphore_signal(barrier, inc=1, device_id=(section - 1, me), device_id_type=MESH)

    @pl.when(jnp.logical_not(is_last))
    def _():
        pl.semaphore_signal(barrier, inc=1, device_id=(section + 1, me), device_id_type=MESH)

    def y_copy(c, to):
        return pltpu.make_async_remote_copy(
            src_ref=y_buf.at[c],
            dst_ref=v_buf.at[c],
            send_sem=y_send.at[c],
            recv_sem=y_recv.at[c],
            device_id=(to, me),
            device_id_type=MESH,
        )

    def up_copy(c, to):
        return pltpu.make_async_remote_copy(
            src_ref=up_buf.at[c],
            dst_ref=cn_buf.at[c, pl.ds(0, rows)],
            send_sem=up_send.at[c],
            recv_sem=up_recv.at[c],
            device_id=(to, me),
            device_id_type=MESH,
        )

    def each_chunk(body):
        for c in range(chunks):
            body(c)

    def gain_of(c):
        return gain_ref[c].astype(jnp.float32)

    def add_d_active(c):
        up = cn_buf[c, pl.ds(0, rows), :]
        dact_buf[...] += jnp.dot(up, w_buf[c], preferred_element_type=jnp.float32)

    for c in range(chunks):
        w_copy(c).wait()

    dact_buf[...] = jnp.zeros_like(dact_buf)

    @pl.when(is_last)
    def _():
        def body(c):
            ct_copy(c).wait()
            add_d_active(c)

        each_chunk(body)

    def squares(c, total):
        @pl.when(is_first)
        def _():
            x_copy(c).wait()

        @pl.when(jnp.logical_not(is_first))
        def _():
            y_copy(c, section - 1).wait_recv()

        wide = v_buf[c].astype(jnp.float32)
        return total + jnp.sum(wide * wide, axis=-1, keepdims=True)

    total = lax.fori_loop(0, chunks, squares, jnp.zeros((rows, 1), jnp.float32), unroll=True)
    r_buf[...] = lax.rsqrt(total / depth + EPSILON)
    hid_buf[...] = jnp.zeros_like(hid_buf)

    def project(c):
        normed = (v_buf[c].astype(jnp.float32) * r_buf[...] * gain_of(c)).astype(jnp.bfloat16)
        cn_buf[c, pl.ds(rows, rows), :] = normed
        hid_buf[...] += jnp.dot(normed, w_buf[c], preferred_element_type=jnp.float32)

    each_chunk(project)
    hidden = hid_buf[...]
    ad_buf[pl.ds(0, rows), :] = (hidden * jax.nn.sigmoid(hidden)).astype(jnp.bfloat16)

    peers = bits + jnp.where(is_first, 0, 1) + jnp.where(is_last, 0, 1)
    pl.semaphore_wait(barrier, peers)

    @pl.when(jnp.logical_not(is_last))
    def _():
        def body(c):
            back = lax.dot_general(
                ad_buf[pl.ds(0, rows), :],
                w_buf[c],
                (((1,), (1,)), ((), ())),
                preferred_element_type=jnp.float32,
            )
            y_buf[c] = (v_buf[c].astype(jnp.float32) + back).astype(jnp.bfloat16)
            y_copy(c, section + 1).start()

        each_chunk(body)

        def arrived(c):
            up_copy(c, section + 1).wait_recv()
            add_d_active(c)

        each_chunk(arrived)

    hidden = hid_buf[...]
    logistic = jax.nn.sigmoid(hidden)
    ad_buf[pl.ds(rows, rows), :] = (
        dact_buf[...] * logistic * (1.0 + hidden * (1.0 - logistic))
    ).astype(jnp.bfloat16)

    per_chunk = width // shard
    plan = part_plan(shard, bits)
    gain_part = len(plan)

    def block_at(order, rel):
        index = 0
        for b, r in zip(order, rel):
            index = index + (my_bit[b] + r * (1 - 2 * my_bit[b])) * (1 << b)
        return index

    def slot_of(rel, step):
        slot = sum(1 << (bits - 1 - s) for s in range(step))
        for r in rel[step + 1 :]:
            step += 1
            slot += r << (bits - 1 - step)
        return slot

    def grad_block(j):
        c, at = j // per_chunk, j % per_chunk
        left = cn_buf[c, :, pl.ds(pl.multiple_of(at * shard, shard), shard)]
        block = lax.dot_general(
            left, ad_buf[...], (((0,), (0,)), ((), ())), preferred_element_type=jnp.float32
        )
        part_w[j] = block.astype(jnp.bfloat16)

    def views(part, j, slot):
        if part == gain_part:
            return part_g.at[j], land_g.at[slot]
        at, size, _ = plan[part]
        return part_w.at[j, pl.ds(at, size)], land_w.at[slot, pl.ds(at, size)]

    def order_of(part):
        return plan[part][2] if part < gain_part else plan[0][2]

    def hop(part, rel):
        order = order_of(part)
        step = rel.index(1)
        slot = slot_of(rel, step)
        source, target = views(part, block_at(order, rel), slot)
        return pltpu.make_async_remote_copy(
            src_ref=source,
            dst_ref=target,
            send_sem=rs_send.at[part, slot],
            recv_sem=rs_recv.at[part, slot],
            device_id=(section, partner[order[step]]),
            device_id_type=MESH,
        )

    def arrivals(part, rel, steps):
        order = order_of(part)
        own = views(part, block_at(order, rel), 0)[0]
        value = own[...].astype(jnp.float32)
        for s in range(steps):
            came = rel[:s] + (1,) + rel[s + 1 :]
            hop(part, came).wait_recv()
            value = value + views(part, 0, slot_of(came, s))[1][...].astype(jnp.float32)
        return own, value

    def combos(count):
        return [tuple((n >> (count - 1 - i)) & 1 for i in range(count)) for n in range((1 << count) - 1, -1, -1)]

    far_combos = combos(bits - 2)

    def grad_group(near):
        def step(n, carry):
            rel = list(near)
            left = (1 << (bits - 2)) - 1 - n
            for i in range(bits - 2):
                rel.append((left // (1 << (bits - 3 - i))) % 2)
            grad_block(block_at(list(range(bits)), rel))
            return carry

        lax.fori_loop(0, 1 << (bits - 2), step, 0, unroll=True)
        for far in far_combos:
            whole = near + far
            for part in range(gain_part):
                rel = tuple(whole[b] for b in order_of(part))
                if rel[0] == 1:
                    hop(part, rel).start()

    grad_group((1, 1))

    def through(c, total):
        dn = lax.dot_general(
            ad_buf[pl.ds(rows, rows), :],
            w_buf[c],
            (((1,), (1,)), ((), ())),
            preferred_element_type=jnp.float32,
        )
        unit = v_buf[c].astype(jnp.float32) * r_buf[...]
        both = dn * unit
        gain_sum = jnp.sum(both, axis=0, keepdims=True)
        pieces = shard // LANES
        at = lax.broadcasted_iota(jnp.int32, part_g.shape[1:], 0)
        for k in range(per_chunk):
            tile = jnp.zeros(part_g.shape[1:], jnp.float32)
            for p in range(pieces):
                piece = gain_sum[:, k * shard + p * LANES : k * shard + (p + 1) * LANES]
                tile = jnp.where(at == p, jnp.broadcast_to(piece, tile.shape), tile)
            part_g[c * per_chunk + k] = tile.astype(jnp.bfloat16)
        scaled = dn * gain_of(c)
        dn_buf[c] = scaled
        return total + jnp.sum(scaled * unit, axis=-1, keepdims=True)

    total = lax.fori_loop(0, chunks, through, jnp.zeros((rows, 1), jnp.float32), unroll=True)

    @pl.when(jnp.logical_not(is_first))
    def _():
        mean = total / depth

        def body(c):
            unit = v_buf[c].astype(jnp.float32) * r_buf[...]
            up = cn_buf[c, pl.ds(0, rows), :].astype(jnp.float32)
            up_buf[c] = (up + r_buf[...] * (dn_buf[c] - unit * mean)).astype(jnp.bfloat16)
            up_copy(c, section - 1).start()

        each_chunk(body)

    grad_group((1, 0))
    grad_group((0, 1))
    grad_group((0, 0))
    for rest in combos(bits - 1):
        hop(gain_part, (1,) + rest).start()

    for step in range(1, bits):
        for rest in combos(bits - 1 - step):
            rel = (0,) * step + (1,) + rest
            for part in range(gain_part + 1):
                own, value = arrivals(part, rel, step)
                own[...] = value.astype(jnp.bfloat16)
                hop(part, rel).start()
    for part in range(gain_part + 1):
        _, value = arrivals(part, (0,) * bits, bits)
        if part < gain_part:
            at, size, _ = plan[part]
            out_w[pl.ds(at, size), :] = value
        else:
            for p in range(shard // LANES):
                out_g[:, p * LANES : (p + 1) * LANES] = value[p : p + 1, :]

    for part in range(gain_part + 1):
        for step in range(bits):
            for rest in combos(bits - 1 - step):
                hop(part, (0,) * step + (1,) + rest).wait_send()

    @pl.when(jnp.logical_not(is_last))
    def _():
        for c in range(chunks):
            y_copy(c, section + 1).wait_send()

    @pl.when(jnp.logical_not(is_first))
    def _():
        for c in range(chunks):
            up_copy(c, section - 1).wait_send()


def on_device(inputs, cotangent, weight, gain):
    sections, replicas = lax.axis_size("section"), lax.axis_size("dp")
    depth, kv = weight.shape[1:]
    rows = inputs.shape[0] * inputs.shape[1]
    width = chunk_of(depth)
    chunks = depth // width
    shard = depth // replicas
    bf16, f32 = jnp.bfloat16, jnp.float32
    dma = pltpu.SemaphoreType.DMA
    parts = len(part_plan(shard, replicas.bit_length() - 1)) + 1
    vmem = pl.BlockSpec(memory_space=pltpu.VMEM)
    hbm = pl.BlockSpec(memory_space=pl.ANY)
    grad_w, grad_g = pl.pallas_call(
        functools.partial(relay_kernel, sections, replicas),
        out_shape=(
            jax.ShapeDtypeStruct((shard, kv), f32),
            jax.ShapeDtypeStruct((1, shard), f32),
        ),
        in_specs=[hbm, hbm, hbm, vmem],
        out_specs=(vmem, vmem),
        scratch_shapes=[
            pltpu.VMEM((chunks, width, kv), bf16),
            pltpu.VMEM((chunks, rows, width), bf16),
            pltpu.VMEM((chunks, 2 * rows, width), bf16),
            pltpu.VMEM((2 * rows, kv), bf16),
            pltpu.VMEM((rows, kv), f32),
            pltpu.VMEM((rows, kv), f32),
            pltpu.VMEM((chunks, rows, width), bf16),
            pltpu.VMEM((chunks, rows, width), bf16),
            pltpu.VMEM((chunks, rows, width), f32),
            pltpu.VMEM((rows, 1), f32),
            pltpu.VMEM((replicas, shard, kv), bf16),
            pltpu.VMEM((replicas - 1, shard, kv), bf16),
            pltpu.VMEM((replicas, 16, LANES), bf16),
            pltpu.VMEM((replicas - 1, 16, LANES), bf16),
            dma((chunks,)),
            dma((chunks,)),
            dma((chunks,)),
            dma((chunks,)),
            dma((chunks,)),
            dma((chunks,)),
            dma((chunks,)),
            dma((parts, replicas - 1)),
            dma((parts, replicas - 1)),
        ],
        compiler_params=pltpu.CompilerParams(
            collective_id=0, has_side_effects=True, vmem_limit_bytes=60 * 1024 * 1024
        ),
        name="relay",
    )(
        inputs.reshape(rows, depth),
        cotangent.reshape(rows, depth),
        weight.reshape(chunks, width, kv),
        gain.reshape(chunks, 1, width),
    )
    return grad_w[None], grad_g


def solution(mesh):
    placed = (
        P(None, "dp", None),
        P(None, "dp", None),
        P("section", None, None),
        P("section", None),
    )
    return jax.shard_map(
        on_device,
        mesh=mesh,
        in_specs=placed,
        out_specs=(P("section", "dp", None), P("section", "dp")),
        check_vma=False,
    )
```

```python
import functools

import jax
import jax.numpy as jnp
from jax import lax
from jax.experimental import pallas as pl
from jax.experimental.pallas import tpu as pltpu
from jax.sharding import PartitionSpec as P

EPSILON = 1e-05
MESH = pl.DeviceIdType.MESH
LANES = 128


def part_plan(shard, bits):
    edges = [shard * e // 256 * 16 for e in (0, 5, 10, 13, 16)]
    near, far = [0, 1], list(range(2, bits))
    orders = [
        near + far,
        near[::-1] + far,
        far[:1] + near + far[1:],
        far[:1] + near[::-1] + far[1:],
    ]
    return [(at, end - at, order) for at, end, order in zip(edges, edges[1:], orders)]


def chunk_of(depth):
    return min(512, depth)


def relay_kernel(
    sections,
    replicas,
    x_hbm,
    ct_hbm,
    w_hbm,
    gain_ref,
    out_w,
    out_g,
    w_buf,
    v_buf,
    cn_buf,
    ad_buf,
    hid_buf,
    dact_buf,
    y_buf,
    up_buf,
    dn_buf,
    r_buf,
    part_w,
    land_w,
    part_g,
    land_g,
    x_sem,
    ct_sem,
    w_sem,
    y_send,
    y_recv,
    up_send,
    up_recv,
    rs_send,
    rs_recv,
):
    section = lax.axis_index("section")
    me = lax.axis_index("dp")
    chunks, rows, width = v_buf.shape
    depth = chunks * width
    bits = replicas.bit_length() - 1
    shard = depth // replicas
    is_first = section == 0
    is_last = section == sections - 1
    my_bit = [(me // (1 << b)) % 2 for b in range(bits)]
    partner = [me + (1 - 2 * my_bit[b]) * (1 << b) for b in range(bits)]

    def x_copy(c):
        return pltpu.make_async_copy(
            x_hbm.at[:, pl.ds(pl.multiple_of(c * width, width), width)], v_buf.at[c], x_sem.at[c]
        )

    def ct_copy(c):
        return pltpu.make_async_copy(
            ct_hbm.at[:, pl.ds(pl.multiple_of(c * width, width), width)],
            cn_buf.at[c, pl.ds(0, rows)],
            ct_sem.at[c],
        )

    def w_copy(c):
        return pltpu.make_async_copy(w_hbm.at[c], w_buf.at[c], w_sem.at[c])

    @pl.when(is_first)
    def _():
        for c in range(chunks):
            x_copy(c).start()

    @pl.when(is_last)
    def _():
        for c in range(chunks):
            ct_copy(c).start()

    for c in range(chunks):
        w_copy(c).start()

    barrier = pltpu.get_barrier_semaphore()
    for b in range(bits):
        pl.semaphore_signal(barrier, inc=1, device_id=(section, partner[b]), device_id_type=MESH)

    @pl.when(jnp.logical_not(is_first))
    def _():
        pl.semaphore_signal(barrier, inc=1, device_id=(section - 1, me), device_id_type=MESH)

    @pl.when(jnp.logical_not(is_last))
    def _():
        pl.semaphore_signal(barrier, inc=1, device_id=(section + 1, me), device_id_type=MESH)

    def y_copy(c, to):
        return pltpu.make_async_remote_copy(
            src_ref=y_buf.at[c],
            dst_ref=v_buf.at[c],
            send_sem=y_send.at[c],
            recv_sem=y_recv.at[c],
            device_id=(to, me),
            device_id_type=MESH,
        )

    def up_copy(c, to):
        return pltpu.make_async_remote_copy(
            src_ref=up_buf.at[c],
            dst_ref=cn_buf.at[c, pl.ds(0, rows)],
            send_sem=up_send.at[c],
            recv_sem=up_recv.at[c],
            device_id=(to, me),
            device_id_type=MESH,
        )

    def each_chunk(body):
        for c in range(chunks):
            body(c)

    def gain_of(c):
        return gain_ref[c].astype(jnp.float32)

    def add_d_active(c):
        up = cn_buf[c, pl.ds(0, rows), :]
        dact_buf[...] += jnp.dot(up, w_buf[c], preferred_element_type=jnp.float32)

    for c in range(chunks):
        w_copy(c).wait()

    dact_buf[...] = jnp.zeros_like(dact_buf)

    @pl.when(is_last)
    def _():
        def body(c):
            ct_copy(c).wait()
            add_d_active(c)

        each_chunk(body)

    def squares(c, total):
        @pl.when(is_first)
        def _():
            x_copy(c).wait()

        @pl.when(jnp.logical_not(is_first))
        def _():
            y_copy(c, section - 1).wait_recv()

        wide = v_buf[c].astype(jnp.float32)
        return total + jnp.sum(wide * wide, axis=-1, keepdims=True)

    total = lax.fori_loop(0, chunks, squares, jnp.zeros((rows, 1), jnp.float32), unroll=True)
    r_buf[...] = lax.rsqrt(total / depth + EPSILON)
    hid_buf[...] = jnp.zeros_like(hid_buf)

    def project(c):
        normed = (v_buf[c].astype(jnp.float32) * r_buf[...] * gain_of(c)).astype(jnp.bfloat16)
        cn_buf[c, pl.ds(rows, rows), :] = normed
        hid_buf[...] += jnp.dot(normed, w_buf[c], preferred_element_type=jnp.float32)

    each_chunk(project)
    hidden = hid_buf[...]
    ad_buf[pl.ds(0, rows), :] = (hidden * jax.nn.sigmoid(hidden)).astype(jnp.bfloat16)

    peers = bits + jnp.where(is_first, 0, 1) + jnp.where(is_last, 0, 1)
    pl.semaphore_wait(barrier, peers)

    @pl.when(jnp.logical_not(is_last))
    def _():
        def body(c):
            back = lax.dot_general(
                ad_buf[pl.ds(0, rows), :],
                w_buf[c],
                (((1,), (1,)), ((), ())),
                preferred_element_type=jnp.float32,
            )
            y_buf[c] = (v_buf[c].astype(jnp.float32) + back).astype(jnp.bfloat16)
            y_copy(c, section + 1).start()

        each_chunk(body)

        def arrived(c):
            up_copy(c, section + 1).wait_recv()
            add_d_active(c)

        each_chunk(arrived)

    hidden = hid_buf[...]
    logistic = jax.nn.sigmoid(hidden)
    ad_buf[pl.ds(rows, rows), :] = (
        dact_buf[...] * logistic * (1.0 + hidden * (1.0 - logistic))
    ).astype(jnp.bfloat16)

    per_chunk = width // shard
    plan = part_plan(shard, bits)
    gain_part = len(plan)

    def block_at(order, rel):
        index = 0
        for b, r in zip(order, rel):
            index = index + (my_bit[b] + r * (1 - 2 * my_bit[b])) * (1 << b)
        return index

    def slot_of(rel, step):
        slot = sum(1 << (bits - 1 - s) for s in range(step))
        for r in rel[step + 1 :]:
            step += 1
            slot += r << (bits - 1 - step)
        return slot

    def grad_block(j):
        c, at = j // per_chunk, j % per_chunk
        left = cn_buf[c, :, pl.ds(pl.multiple_of(at * shard, shard), shard)]
        block = lax.dot_general(
            left, ad_buf[...], (((0,), (0,)), ((), ())), preferred_element_type=jnp.float32
        )
        part_w[j] = block.astype(jnp.bfloat16)

    def views(part, j, slot):
        if part == gain_part:
            return part_g.at[j], land_g.at[slot]
        at, size, _ = plan[part]
        return part_w.at[j, pl.ds(at, size)], land_w.at[slot, pl.ds(at, size)]

    def order_of(part):
        return plan[part][2] if part < gain_part else plan[0][2]

    def hop(part, rel):
        order = order_of(part)
        step = rel.index(1)
        slot = slot_of(rel, step)
        source, target = views(part, block_at(order, rel), slot)
        return pltpu.make_async_remote_copy(
            src_ref=source,
            dst_ref=target,
            send_sem=rs_send.at[part, slot],
            recv_sem=rs_recv.at[part, slot],
            device_id=(section, partner[order[step]]),
            device_id_type=MESH,
        )

    def arrivals(part, rel, steps):
        order = order_of(part)
        own = views(part, block_at(order, rel), 0)[0]
        value = own[...].astype(jnp.float32)
        for s in range(steps):
            came = rel[:s] + (1,) + rel[s + 1 :]
            hop(part, came).wait_recv()
            value = value + views(part, 0, slot_of(came, s))[1][...].astype(jnp.float32)
        return own, value

    def combos(count):
        return [tuple((n >> (count - 1 - i)) & 1 for i in range(count)) for n in range((1 << count) - 1, -1, -1)]

    far_combos = combos(bits - 2)

    def grad_group(near):
        def step(n, carry):
            rel = list(near)
            left = (1 << (bits - 2)) - 1 - n
            for i in range(bits - 2):
                rel.append((left // (1 << (bits - 3 - i))) % 2)
            grad_block(block_at(list(range(bits)), rel))
            return carry

        lax.fori_loop(0, 1 << (bits - 2), step, 0, unroll=True)
        for far in far_combos:
            whole = near + far
            for part in range(gain_part):
                rel = tuple(whole[b] for b in order_of(part))
                if rel[0] == 1:
                    hop(part, rel).start()

    grad_group((1, 1))

    def through(c, total):
        dn = lax.dot_general(
            ad_buf[pl.ds(rows, rows), :],
            w_buf[c],
            (((1,), (1,)), ((), ())),
            preferred_element_type=jnp.float32,
        )
        unit = v_buf[c].astype(jnp.float32) * r_buf[...]
        both = dn * unit
        gain_sum = jnp.sum(both, axis=0, keepdims=True)
        pieces = shard // LANES
        at = lax.broadcasted_iota(jnp.int32, part_g.shape[1:], 0)
        for k in range(per_chunk):
            tile = jnp.zeros(part_g.shape[1:], jnp.float32)
            for p in range(pieces):
                piece = gain_sum[:, k * shard + p * LANES : k * shard + (p + 1) * LANES]
                tile = jnp.where(at == p, jnp.broadcast_to(piece, tile.shape), tile)
            part_g[c * per_chunk + k] = tile.astype(jnp.bfloat16)
        scaled = dn * gain_of(c)
        dn_buf[c] = scaled
        return total + jnp.sum(scaled * unit, axis=-1, keepdims=True)

    total = lax.fori_loop(0, chunks, through, jnp.zeros((rows, 1), jnp.float32), unroll=True)

    @pl.when(jnp.logical_not(is_first))
    def _():
        mean = total / depth

        def body(c):
            unit = v_buf[c].astype(jnp.float32) * r_buf[...]
            up = cn_buf[c, pl.ds(0, rows), :].astype(jnp.float32)
            up_buf[c] = (up + r_buf[...] * (dn_buf[c] - unit * mean)).astype(jnp.bfloat16)
            up_copy(c, section - 1).start()

        each_chunk(body)

    grad_group((1, 0))
    grad_group((0, 1))
    grad_group((0, 0))
    for rest in combos(bits - 1):
        hop(gain_part, (1,) + rest).start()

    for step in range(1, bits):
        for rest in combos(bits - 1 - step):
            rel = (0,) * step + (1,) + rest
            for part in range(gain_part + 1):
                own, value = arrivals(part, rel, step)
                own[...] = value.astype(jnp.bfloat16)
                hop(part, rel).start()
    for part in range(gain_part + 1):
        _, value = arrivals(part, (0,) * bits, bits)
        if part < gain_part:
            at, size, _ = plan[part]
            out_w[pl.ds(at, size), :] = value
        else:
            for p in range(shard // LANES):
                out_g[:, p * LANES : (p + 1) * LANES] = value[p : p + 1, :]

    for part in range(gain_part + 1):
        for step in range(bits):
            for rest in combos(bits - 1 - step):
                hop(part, (0,) * step + (1,) + rest).wait_send()

    @pl.when(jnp.logical_not(is_last))
    def _():
        for c in range(chunks):
            y_copy(c, section + 1).wait_send()

    @pl.when(jnp.logical_not(is_first))
    def _():
        for c in range(chunks):
            up_copy(c, section - 1).wait_send()


def settle_kernel(grad_w, grad_g, out_w, out_g):
    out_w[0] = grad_w[...]
    out_g[...] = grad_g[...]


def on_device(inputs, cotangent, weight, gain):
    sections, replicas = lax.axis_size("section"), lax.axis_size("dp")
    depth, kv = weight.shape[1:]
    rows = inputs.shape[0] * inputs.shape[1]
    width = chunk_of(depth)
    chunks = depth // width
    shard = depth // replicas
    bf16, f32 = jnp.bfloat16, jnp.float32
    dma = pltpu.SemaphoreType.DMA
    parts = len(part_plan(shard, replicas.bit_length() - 1)) + 1
    vmem = pl.BlockSpec(memory_space=pltpu.VMEM)
    hbm = pl.BlockSpec(memory_space=pl.ANY)
    grad_w, grad_g = pl.pallas_call(
        functools.partial(relay_kernel, sections, replicas),
        out_shape=(
            jax.ShapeDtypeStruct((shard, kv), f32),
            jax.ShapeDtypeStruct((1, shard), f32),
        ),
        in_specs=[hbm, hbm, hbm, vmem],
        out_specs=(vmem, vmem),
        scratch_shapes=[
            pltpu.VMEM((chunks, width, kv), bf16),
            pltpu.VMEM((chunks, rows, width), bf16),
            pltpu.VMEM((chunks, 2 * rows, width), bf16),
            pltpu.VMEM((2 * rows, kv), bf16),
            pltpu.VMEM((rows, kv), f32),
            pltpu.VMEM((rows, kv), f32),
            pltpu.VMEM((chunks, rows, width), bf16),
            pltpu.VMEM((chunks, rows, width), bf16),
            pltpu.VMEM((chunks, rows, width), f32),
            pltpu.VMEM((rows, 1), f32),
            pltpu.VMEM((replicas, shard, kv), bf16),
            pltpu.VMEM((replicas - 1, shard, kv), bf16),
            pltpu.VMEM((replicas, 16, LANES), bf16),
            pltpu.VMEM((replicas - 1, 16, LANES), bf16),
            dma((chunks,)),
            dma((chunks,)),
            dma((chunks,)),
            dma((chunks,)),
            dma((chunks,)),
            dma((chunks,)),
            dma((chunks,)),
            dma((parts, replicas - 1)),
            dma((parts, replicas - 1)),
        ],
        compiler_params=pltpu.CompilerParams(
            collective_id=0, has_side_effects=True, vmem_limit_bytes=60 * 1024 * 1024
        ),
        name="relay",
    )(
        inputs.reshape(rows, depth),
        cotangent.reshape(rows, depth),
        weight.reshape(chunks, width, kv),
        gain.reshape(chunks, 1, width),
    )
    return pl.pallas_call(
        settle_kernel,
        out_shape=(
            jax.ShapeDtypeStruct((1, shard, kv), f32),
            jax.ShapeDtypeStruct((1, shard), f32),
        ),
        in_specs=[vmem, vmem],
        out_specs=(vmem, vmem),
        name="settle",
    )(grad_w, grad_g)


def solution(mesh):
    placed = (
        P(None, "dp", None),
        P(None, "dp", None),
        P("section", None, None),
        P("section", None),
    )
    return jax.shard_map(
        on_device,
        mesh=mesh,
        in_specs=placed,
        out_specs=(P("section", "dp", None), P("section", "dp")),
        check_vma=False,
    )
```
